1024 devices in a mesh: seq: 64 (over z, core), tp: 16 (over y, x).
Axes of the slice: x: 4, y: 4, z: 32, core: 2. Of those that a mesh axis runs over, the one named last changes fastest.
Arguments:
- hidden: bfloat16 [16384, 7168], P(('seq', 'tp')), may hold values from -6 to 6
- next_ids: int32 [16384], replicated, may hold values from 0 to 65535, as said below
- live_mask: int32 [16384], P('seq'), may hold values 0 or 1
- emb_table: bfloat16 [65536, 7168], P('seq', 'tp'), may hold values from -90 to 90
- gain_hidden: float32 [7168], replicated, may hold values from 0.25 to 1.75
- gain_embed: float32 [7168], replicated, may hold values from 0.25 to 1.75
- projection: bfloat16 [14336, 3584], P(None, 'tp'), may hold values from -2 to 2
- target: bfloat16 [16384, 3584], P('seq', 'tp'), may hold values from -6 to 6
Outputs:
- projected: bfloat16 [16384, 3584], P('seq', 'tp')
- table_grad: bfloat16 [65536, 7168], P('seq', 'tp')
The draws below stay inside these ranges and needn't reach their ends.
Inputs may be any that keep to these rules, and one draw needn't show every extreme that they name: `next_ids`: positions come in aligned blocks of 256, one block for each index of seq. In every block at most 8 ids lie in any one range of 1024 ids that starts at a multiple of 1024, and in every block exactly 8 lie in one such range.
All inputs are finite; a program needn't handle non-finite values. No bound on the sum of `live_mask` on one device may be relied on, other than what follows from the above.
Results may differ from the reference program's by a relative error of at most 0.019.
Values may be sent and summed in bfloat16 or wider, within the bound.
No kernel may reach another device: no remote copies, remote signals or barrier semaphores. Data moves between devices by JAX's collectives and lax.ppermute only.
A program may use at most 64 MiB of HBM per device.

```python
import math
import jax
import jax.numpy as jnp
from jax import lax

D = 7168
DOUT = 3584
VOCAB = 65536
TOK_SEQ = 256
TOKENS = 16384
N_TP = 16


def draw_next_ids(key, part):
    key = jax.random.fold_in(key, 11)
    groups = TOKENS // TOK_SEQ
    capacity = 2 * TOK_SEQ // groups
    row_count = VOCAB // groups

    def one_block(block_key):
        key_order, key_rest, key_shuffle, key_rows = jax.random.split(block_key, 4)
        owner_order = jax.random.permutation(key_order, groups)
        others = jax.random.permutation(key_rest, groups * capacity - capacity)[:TOK_SEQ - capacity] + capacity
        slots = jnp.concatenate([jnp.arange(capacity, dtype=jnp.int32), others.astype(jnp.int32)])
        owners = owner_order[slots // capacity]
        owners = jax.random.permutation(key_shuffle, owners)
        offsets = jax.random.randint(key_rows, (TOK_SEQ,), 0, row_count)
        return (owners * row_count + offsets).astype(jnp.int32)
    blocks = jax.vmap(one_block)(jax.random.split(key, groups))
    return blocks.reshape(TOKENS).astype(jnp.int32)


def draw_emb_table(key, part):
    key = jax.random.fold_in(key, 23)
    key_vals, key_cols = jax.random.split(key, 2)
    position = jnp.arange(D, dtype=jnp.float32) / D
    rough = jnp.exp(jax.random.uniform(key_cols, (D,), jnp.float32, -0.35, 0.35))
    column_scale = jnp.exp(math.log(10.0) * position) * rough
    values = jnp.clip(jax.random.normal(key_vals, (VOCAB, D), jnp.float32), -4.0, 4.0)
    return (values * column_scale[None, :]).astype(jnp.bfloat16)


def draw_projection(key, part):
    key = jax.random.fold_in(key, 37)
    key_top, key_low, key_cols = jax.random.split(key, 3)
    upper = jnp.clip(jax.random.normal(key_top, (D, DOUT), jnp.float32), -4.0, 4.0)
    lower = jnp.clip(jax.random.normal(key_low, (D, DOUT), jnp.float32), -4.0, 4.0)
    rise = math.log(3.0)
    position = jnp.arange(DOUT, dtype=jnp.float32) / DOUT
    rough = jnp.exp(jax.random.uniform(key_cols, (DOUT,), jnp.float32, -0.2, 0.2))
    column_scale = jnp.exp(rise * position) * rough
    whole = jnp.concatenate([upper, lower * column_scale[None, :]], axis=0)
    return (whole * (1.0 / math.sqrt(2.0 * D))).astype(jnp.bfloat16)


def with_ends(drawn, stream_key, smallest, top_value):
    longest = drawn.shape.index(max(drawn.shape))
    spots = []
    for shift in (0, 1):
        where = [jax.random.randint(jax.random.fold_in(stream_key, axis), (), 0, length) for axis, length in enumerate(drawn.shape)]
        where[longest] = (where[longest] + shift) % drawn.shape[longest]
        spots.append(tuple(where))
    return drawn.at[spots[0]].set(smallest).at[spots[1]].set(top_value)


def levels(key, shape, cuts, low, largest):
    def one(dim, shards_of):
        steps = jax.random.uniform(jax.random.fold_in(jax.random.fold_in(key, 6), dim), (shards_of,), jnp.float32, low / len(cuts), largest / len(cuts))
        return jnp.repeat(jnp.exp(steps), shape[dim] // shards_of).reshape((-1,) + (1,) * (len(shape) - dim - 1))

    gain = one(*cuts[0])
    for cut in cuts[1:]:
        gain = gain * one(*cut)
    return gain


def gaussian(rng, shape, scale, most, cuts=(), kind=jnp.bfloat16):
    entries = scale * jax.random.normal(rng, shape, jnp.float32)
    if cuts:
        entries = entries * levels(rng, shape, cuts, -0.22, 0.18)
    return jnp.clip(entries, -most, most).astype(kind)


def setup_inputs(seed: int = 0) -> dict:
    splits = jax.random.split(jax.random.key(seed), 9)
    hidden = gaussian(splits[0], (TOKENS, D), 1.0, 6.0, ((0, 1024),))
    next_ids = draw_next_ids(jax.random.fold_in(splits[8], 71), 0)
    live_mask = with_ends((jax.random.randint(splits[2], (TOKENS,), 0, 16) < 15).astype(jnp.int32), jax.random.fold_in(splits[2], 1), 0, 1)
    emb_table = draw_emb_table(jax.random.fold_in(splits[8], 71), 0)
    gain_hidden = jnp.clip(1.0 + 0.15 * jax.random.normal(splits[4], (D,), jnp.float32), 0.25, 1.75)
    gain_embed = jnp.clip(1.0 + 0.15 * jax.random.normal(splits[5], (D,), jnp.float32), 0.25, 1.75)
    projection = draw_projection(jax.random.fold_in(splits[8], 71), 0)
    target = gaussian(splits[7], (TOKENS, DOUT), 1.0, 6.0, ((0, 64), (1, 16)))
    return dict(hidden=hidden, next_ids=next_ids, live_mask=live_mask, emb_table=emb_table, gain_hidden=gain_hidden, gain_embed=gain_embed, projection=projection, target=target)


def rms_scale(values):
    return lax.rsqrt(lax.optimization_barrier(jnp.mean(values * values, axis=-1, keepdims=True)) + 1e-06)

def reference(hidden, next_ids, live_mask, emb_table, gain_hidden, gain_embed, projection, target):
    width = hidden.shape[1]
    hidden_f32 = hidden.astype(jnp.float32)
    hid_norm = (hidden_f32 * rms_scale(hidden_f32) * gain_hidden).astype(jnp.bfloat16)
    keep_rows = live_mask.astype(jnp.float32)[:, None]
    emb_rows = emb_table[next_ids].astype(jnp.float32) * keep_rows
    scale = rms_scale(emb_rows)
    emb_norm = (emb_rows * scale * gain_embed).astype(jnp.bfloat16)
    combined = jnp.dot(hid_norm, projection[:width], preferred_element_type=jnp.float32)
    combined = combined + jnp.dot(emb_norm, projection[width:], preferred_element_type=jnp.float32)
    projected = combined.astype(jnp.bfloat16)
    upstream = (combined - target.astype(jnp.float32)).astype(jnp.bfloat16)
    columns = projection.shape[1] // N_TP
    feature_grad = jnp.zeros((hidden.shape[0], width), jnp.float32)
    for block in range(N_TP):
        partial_sum = lax.dot_general(upstream[:, block * columns:(block + 1) * columns], projection[width:, block * columns:(block + 1) * columns], (((1,), (1,)), ((), ())), preferred_element_type=jnp.float32)
        partial_sum = lax.optimization_barrier(partial_sum.astype(jnp.bfloat16))
        feature_grad = feature_grad + partial_sum.astype(jnp.float32)
    curvature = lax.optimization_barrier(jnp.sum(emb_rows * gain_embed * feature_grad, axis=1, keepdims=True))
    emb_grad = keep_rows * (scale * gain_embed * feature_grad - scale * scale * scale * curvature / width * emb_rows)
    emb_grad = emb_grad.astype(jnp.bfloat16)
    table_grad = jnp.zeros((VOCAB, width), jnp.float32).at[next_ids].add(emb_grad.astype(jnp.float32))
    return (projected, table_grad.astype(jnp.bfloat16))
```

```python
import jax
import jax.numpy as jnp
from jax import lax
from jax.sharding import PartitionSpec as P

BF16 = jnp.bfloat16
F32 = jnp.float32
I32 = jnp.int32
SIDE = 4
PIECES = 16


def contract(left, right, dims):
    return lax.dot_general(left, right, ((dims[:1], dims[1:]), ((), ())), preferred_element_type=F32)


def split_rows(row):
    high = row.astype(BF16)
    rest = row - high.astype(F32)
    middle = rest.astype(BF16)
    low = (rest - middle.astype(F32)).astype(BF16)
    pieces = jnp.concatenate([high, middle, low], axis=0)
    return jnp.pad(pieces, ((0, PIECES - 3), (0, 0)))


def join_rows(rows):
    return jnp.sum(rows.astype(F32), axis=(0, 1))[None, :]


def along_x(value):
    groups = [[SIDE * y + x for x in range(SIDE)] for y in range(SIDE)]
    return lax.all_to_all(value, "tp", 0, 0, tiled=True, axis_index_groups=groups)


def along_y(value):
    groups = [[SIDE * y + x for y in range(SIDE)] for x in range(SIDE)]
    return lax.all_to_all(value, "tp", 0, 0, tiled=True, axis_index_groups=groups)


def to_all(value):
    return jnp.broadcast_to(value, (SIDE,) + value.shape)


def local(hidden, next_ids, live_mask, emb_table, gain_hidden, gain_embed, projection, target):
    width = hidden.shape[1]
    groups = lax.axis_size("seq")
    my_group = lax.axis_index("seq")
    place_tp = lax.axis_index("tp")
    my_y = place_tp // SIDE
    tokens = live_mask.shape[0]
    capacity = 2 * tokens // groups
    slots = groups * capacity
    row_count, local_width = emb_table.shape
    columns = projection.shape[1]
    quarter = width // SIDE

    hidden_f32 = hidden.astype(F32)
    hidden_scale = lax.rsqrt(jnp.mean(hidden_f32 * hidden_f32, axis=-1, keepdims=True) + 1e-06)
    hid_norm = (hidden_f32 * hidden_scale * gain_hidden).astype(BF16)
    hid_all = lax.all_gather(hid_norm, "tp", axis=0, tiled=True)

    proj_t = projection.T

    def piece(y):
        return lax.dynamic_slice(proj_t, (0, width + y * quarter), (columns, quarter))

    weights = jnp.zeros((SIDE, columns, quarter), BF16)
    weights = lax.dynamic_update_slice(weights, piece(my_y)[None], (my_y, 0, 0))
    for step in range(1, SIDE):
        moved = lax.ppermute(
            piece((my_y + step) % SIDE),
            "tp",
            [(SIDE * y + x, SIDE * ((y + step) % SIDE) + x) for y in range(SIDE) for x in range(SIDE)],
        )
        weights = lax.dynamic_update_slice(weights, moved[None], ((my_y - step) % SIDE, 0, 0))
    weights = weights.reshape(SIDE * columns, quarter)

    ids_all = next_ids.reshape(groups, tokens)
    mine = ids_all // row_count == my_group
    token = jnp.arange(tokens, dtype=I32)
    upto = (token[:, None] <= token[None, :]).astype(BF16)
    rank_all = contract(mine.astype(BF16), upto, (1, 0)).astype(I32) - 1
    hit = mine[:, :, None] & (rank_all[:, :, None] == jnp.arange(capacity, dtype=I32))
    local_ids = ids_all - my_group * row_count
    row_of_slot = jnp.sum(jnp.where(hit, local_ids[:, :, None] + 1, 0), axis=1).reshape(slots) - 1
    pick = (row_of_slot[:, None] == jnp.arange(row_count, dtype=I32)[None, :]).astype(BF16)
    outgoing = contract(pick, emb_table, (1, 0)).astype(BF16).reshape(groups, capacity, local_width)
    fetched = lax.all_to_all(outgoing, "seq", split_axis=0, concat_axis=0, tiled=True)

    ids_mine = lax.dynamic_index_in_dim(ids_all, my_group, 0, keepdims=False)
    owner = ids_mine // row_count
    earlier = (owner[:, None] == owner[None, :]) & (token[:, None] < token[None, :])
    slot = owner * capacity + jnp.sum(earlier.astype(I32), axis=0)
    place = (jnp.arange(slots, dtype=I32)[:, None] == slot[None, :]) & (live_mask[None, :] != 0)
    place = place.astype(BF16)

    emb = contract(fetched.reshape(slots, local_width), place, (0, 0))
    gain = lax.dynamic_slice_in_dim(gain_embed, place_tp * local_width, local_width)[:, None]
    square_part = jnp.sum(emb * emb, axis=0, keepdims=True)
    got = along_x(to_all(jnp.concatenate([(emb * gain).astype(BF16), split_rows(square_part)], axis=0)))
    square_part = join_rows(got[:, local_width:])
    partial = contract(weights, got[:, :local_width].reshape(quarter, tokens), (1, 0)).astype(BF16)
    partial = partial.reshape(SIDE, columns, tokens)
    got = along_y(jnp.concatenate([partial, to_all(split_rows(square_part))], axis=1))
    emb_raw = jnp.sum(got[:, :columns].astype(F32), axis=0)
    scale = lax.rsqrt(join_rows(got[:, columns:]) / width + 1e-06)

    hid_part = contract(proj_t[:, :width], hid_all, (1, 1))
    combined = hid_part + emb_raw * scale
    projected = combined.astype(BF16)
    upstream = (combined - target.T.astype(F32)).astype(BF16)
    curve_part = jnp.sum(upstream.astype(F32) * emb_raw, axis=0, keepdims=True)
    got = along_y(to_all(jnp.concatenate([upstream, split_rows(curve_part)], axis=0)))
    curve_part = join_rows(got[:, columns:])
    partial = contract(weights, got[:, :columns].reshape(SIDE * columns, tokens), (0, 0)).astype(BF16)
    partial = partial.reshape(SIDE, local_width, tokens)
    got = along_x(jnp.concatenate([partial, to_all(split_rows(curve_part))], axis=1))
    feature_grad = jnp.sum(got[:, :local_width].astype(F32), axis=0)
    curvature = join_rows(got[:, local_width:])

    emb_grad = scale * gain * feature_grad - scale * scale * scale * curvature / width * emb
    returned = contract(place, emb_grad.astype(BF16), (1, 1)).astype(BF16)
    arrived = lax.all_to_all(
        returned.reshape(groups, capacity, local_width), "seq", split_axis=0, concat_axis=0, tiled=True
    )
    table_grad = contract(arrived.reshape(slots, local_width), pick, (0, 0)).astype(BF16)
    return (projected.T, table_grad.T)


def solution(mesh):
    return jax.shard_map(
        local,
        mesh=mesh,
        in_specs=(
            P(("seq", "tp"), None),
            P(),
            P("seq"),
            P("seq", "tp"),
            P(),
            P(),
            P(None, "tp"),
            P("seq", "tp"),
        ),
        out_specs=(P("seq", "tp"), P("seq", "tp")),
        check_vma=False,
    )
```

```python
import jax
import jax.numpy as jnp
from jax import lax
from jax.sharding import PartitionSpec as P

BF16 = jnp.bfloat16
F32 = jnp.float32
I32 = jnp.int32
SIDE = 4
PIECES = 16


def contract(left, right, dims):
    return lax.dot_general(left, right, ((dims[:1], dims[1:]), ((), ())), preferred_element_type=F32)


def split_rows(row):
    high = row.astype(BF16)
    rest = row - high.astype(F32)
    middle = rest.astype(BF16)
    low = (rest - middle.astype(F32)).astype(BF16)
    pieces = jnp.concatenate([high, middle, low], axis=0)
    return jnp.pad(pieces, ((0, PIECES - 3), (0, 0)))


def join_rows(row, messages, start):
    return row + sum(jnp.sum(m[start:].astype(F32), axis=0, keepdims=True) for m in messages)


def shift_x(value, step):
    pairs = [(SIDE * y + x, SIDE * y + (x + step) % SIDE) for y in range(SIDE) for x in range(SIDE)]
    return lax.ppermute(value, "tp", pairs)


def shift_y(value, step):
    pairs = [(SIDE * y + x, SIDE * ((y + step) % SIDE) + x) for y in range(SIDE) for x in range(SIDE)]
    return lax.ppermute(value, "tp", pairs)


def gather_xy(value, over_y):
    side = range(SIDE)
    if over_y:
        groups = [[SIDE * y + x for y in side] for x in side]
    else:
        groups = [[SIDE * y + x for x in side] for y in side]
    return lax.all_gather(value, "tp", axis=0, tiled=True, axis_index_groups=groups)


def at(stack, index):
    return lax.dynamic_index_in_dim(stack, index, 0, keepdims=False)


def exchange_rows(left, right):
    groups = lax.axis_size("seq")
    both = jnp.concatenate([left, right], axis=0).astype(BF16).T
    both = both.reshape(groups, both.shape[0] // groups, both.shape[1])
    moved = lax.all_to_all(both, "seq", split_axis=0, concat_axis=0, tiled=True)
    return moved.reshape(-1, moved.shape[2])


def local(hidden, next_ids, live_mask, emb_table, gain_hidden, gain_embed, projection, target):
    width = hidden.shape[1]
    groups = lax.axis_size("seq")
    my_group = lax.axis_index("seq")
    place_tp = lax.axis_index("tp")
    my_y = place_tp // SIDE
    my_x = place_tp % SIDE
    tokens = live_mask.shape[0]
    capacity = 2 * tokens // groups
    slots = groups * capacity
    row_count, local_width = emb_table.shape
    columns = projection.shape[1]
    quarter = width // SIDE

    hidden_f32 = hidden.astype(F32)
    hidden_scale = lax.rsqrt(jnp.mean(hidden_f32 * hidden_f32, axis=-1, keepdims=True) + 1e-06)
    hid_norm = (hidden_f32 * hidden_scale * gain_hidden).astype(BF16)
    hid_all = gather_xy(gather_xy(hid_norm, True), False)

    proj_t = projection.T

    def piece(y):
        return lax.dynamic_slice(proj_t, (0, width + y * quarter), (columns, quarter))

    weights = jnp.zeros((SIDE, columns, quarter), BF16)
    for step in range(SIDE):
        block = shift_y(piece((my_y + step) % SIDE), step) if step else piece(my_y)
        weights = lax.dynamic_update_slice(weights, block[None], (step, 0, 0))
    weights = weights.reshape(SIDE * columns, quarter)

    ids_all = next_ids.reshape(groups, tokens)
    mine = ids_all // row_count == my_group
    token = jnp.arange(tokens, dtype=I32)
    upto = (token[:, None] <= token[None, :]).astype(BF16)
    rank_all = contract(mine.astype(BF16), upto, (1, 0)).astype(I32) - 1
    local_ids = ids_all - my_group * row_count
    half = capacity // 2
    row = jnp.arange(row_count, dtype=I32)

    def picked(first):
        ranks = first + jnp.arange(half, dtype=I32)
        hit = mine[:, None, :] & (rank_all[:, None, :] == ranks[None, :, None])
        rows = jnp.sum(jnp.where(hit, local_ids[:, None, :] + 1, 0), axis=2).reshape(slots // 2) - 1
        return (row[:, None] == rows[None, :]).astype(BF16)

    pick_left, pick_right = picked(0), picked(half)
    table_t = emb_table.T
    fetched = exchange_rows(contract(table_t, pick_left, (1, 0)), contract(table_t, pick_right, (1, 0)))

    ids_mine = lax.dynamic_index_in_dim(ids_all, my_group, 0, keepdims=False)
    owner = ids_mine // row_count
    earlier = (owner[:, None] == owner[None, :]) & (token[:, None] < token[None, :])
    rank = jnp.sum(earlier.astype(I32), axis=0)
    slot = owner * half + rank % half
    place = (jnp.arange(slots // 2, dtype=I32)[:, None] == slot[None, :]) & (live_mask[None, :] != 0)
    place_left = (place & (rank < half)[None, :]).astype(BF16)
    place_right = (place & (rank >= half)[None, :]).astype(BF16)

    emb = contract(fetched, place_left, (0, 0))[:local_width] + contract(fetched, place_right, (0, 0))[local_width:]
    gain = lax.dynamic_slice_in_dim(gain_embed, place_tp * local_width, local_width)[:, None]
    squares = jnp.sum(emb * emb, axis=0, keepdims=True)
    message = jnp.concatenate([(emb * gain).astype(BF16), split_rows(squares)], axis=0)
    got = [shift_x(message, step) for step in range(1, SIDE)]
    squares = join_rows(squares, got, local_width)
    features = jnp.zeros((SIDE, local_width, tokens), BF16)
    for step, part in enumerate([message] + got):
        features = lax.dynamic_update_slice(
            features, part[None, :local_width], ((my_x - step) % SIDE, 0, 0)
        )
    partial = contract(weights, features.reshape(quarter, tokens), (1, 0)).reshape(SIDE, columns, tokens)
    square_rows = split_rows(squares)
    partial, hid_all = lax.optimization_barrier((partial, hid_all))
    got = [
        shift_y(jnp.concatenate([partial[step].astype(BF16), square_rows], axis=0), -step)
        for step in range(1, SIDE)
    ]
    hid_part = contract(hid_all, proj_t[:, :width], (1, 1))
    hid_part = hid_part.reshape(SIDE, SIDE, tokens // (SIDE * SIDE), columns)
    hid_part = lax.optimization_barrier(hid_part.transpose(1, 0, 2, 3).reshape(tokens, columns).T)
    emb_raw = partial[0] + sum(part[:columns].astype(F32) for part in got)
    scale = lax.rsqrt(join_rows(squares, got, columns) / width + 1e-06)

    combined = hid_part + emb_raw * scale
    projected = combined.astype(BF16)
    upstream = (combined - target.T.astype(F32)).astype(BF16)
    curve = jnp.sum(upstream.astype(F32) * emb_raw, axis=0, keepdims=True)
    message = jnp.concatenate([upstream, split_rows(curve)], axis=0)
    got = [shift_y(message, step) for step in range(1, SIDE)]
    curve = join_rows(curve, got, columns)
    upstream_all = jnp.concatenate([part[:columns] for part in [message] + got], axis=0)
    partial = contract(weights, upstream_all, (0, 0)).astype(BF16).reshape(SIDE, local_width, tokens)
    curve_rows = split_rows(curve)
    got = [
        shift_x(jnp.concatenate([at(partial, (my_x - step) % SIDE), curve_rows], axis=0), -step)
        for step in range(1, SIDE)
    ]
    feature_grad = at(partial, my_x).astype(F32) + sum(part[:local_width].astype(F32) for part in got)
    curvature = join_rows(curve, got, local_width)

    emb_grad = scale * gain * feature_grad - scale * scale * scale * curvature / width * emb
    emb_grad = emb_grad.astype(BF16)
    arrived = exchange_rows(contract(emb_grad, place_left, (1, 1)), contract(emb_grad, place_right, (1, 1)))
    table_grad = (
        contract(arrived, pick_left, (0, 1))[:local_width] + contract(arrived, pick_right, (0, 1))[local_width:]
    ).astype(BF16)
    return (projected.T, table_grad.T)


def solution(mesh):
    return jax.shard_map(
        local,
        mesh=mesh,
        in_specs=(
            P(("seq", "tp"), None),
            P(),
            P("seq"),
            P("seq", "tp"),
            P(),
            P(),
            P(None, "tp"),
            P("seq", "tp"),
        ),
        out_specs=(P("seq", "tp"), P("seq", "tp")),
        check_vma=False,
    )
```

```python
import functools

import jax
import jax.numpy as jnp
from jax import lax
from jax.experimental import pallas as pl
from jax.sharding import PartitionSpec as P

BF16 = jnp.bfloat16
F32 = jnp.float32
I32 = jnp.int32
SIDE = 4
PIECES = 16
COST = 1000000
BYTES = 400000000


def contract(left, right, dims):
    return lax.dot_general(left, right, ((dims[:1], dims[1:]), ((), ())), preferred_element_type=F32)


def split_rows(row):
    high = row.astype(BF16)
    rest = row - high.astype(F32)
    middle = rest.astype(BF16)
    low = (rest - middle.astype(F32)).astype(BF16)
    pieces = jnp.concatenate([high, middle, low], axis=0)
    return jnp.pad(pieces, ((0, PIECES - 3), (0, 0)))


def join_rows(rows):
    return jnp.sum(rows.astype(F32), axis=(0, 1))[None, :]


def place_kernel(half, owner_row, owner_column, live, left, right):
    tokens = owner_row.shape[1]
    below = lax.broadcasted_iota(I32, (tokens, tokens), 0)
    across = lax.broadcasted_iota(I32, (tokens, tokens), 1)
    earlier = (owner_column[...] == owner_row[...]) & (below < across)
    rank = jnp.sum(earlier.astype(I32), axis=0, keepdims=True)
    base = owner_row[...] * half
    row = lax.broadcasted_iota(I32, left.shape, 0)
    used = live[...] != 0
    left[...] = jnp.where((row == base + rank) & (rank < half) & used, 1.0, 0.0).astype(BF16)
    right[...] = jnp.where((row == base + rank - half) & (rank >= half) & used, 1.0, 0.0).astype(BF16)


def placed(owner, live, half, slots):
    tokens = owner.shape[0]
    return pl.pallas_call(
        functools.partial(place_kernel, half),
        out_shape=[jax.ShapeDtypeStruct((slots // 2, tokens), BF16)] * 2,
        cost_estimate=pl.CostEstimate(flops=COST, bytes_accessed=BYTES, transcendentals=0),
    )(owner[None, :], owner[:, None], live[None, :])


def along_x(value):
    groups = [[SIDE * y + x for x in range(SIDE)] for y in range(SIDE)]
    return lax.all_to_all(value, "tp", 0, 0, tiled=True, axis_index_groups=groups)


def along_y(value):
    groups = [[SIDE * y + x for y in range(SIDE)] for x in range(SIDE)]
    return lax.all_to_all(value, "tp", 0, 0, tiled=True, axis_index_groups=groups)


def to_all(value):
    return jnp.broadcast_to(value, (SIDE,) + value.shape)


def exchange_rows(left, right):
    groups = lax.axis_size("seq")
    both = jnp.concatenate([left, right], axis=0).astype(BF16).T
    both = both.reshape(groups, both.shape[0] // groups, both.shape[1])
    moved = lax.all_to_all(both, "seq", split_axis=0, concat_axis=0, tiled=True)
    return moved.reshape(-1, moved.shape[2])


def local(hidden, next_ids, live_mask, emb_table, gain_hidden, gain_embed, projection, target):
    width = hidden.shape[1]
    groups = lax.axis_size("seq")
    my_group = lax.axis_index("seq")
    place_tp = lax.axis_index("tp")
    my_y = place_tp // SIDE
    tokens = live_mask.shape[0]
    capacity = 2 * tokens // groups
    slots = groups * capacity
    row_count, local_width = emb_table.shape
    columns = projection.shape[1]
    quarter = width // SIDE

    hidden_f32 = hidden.astype(F32)
    hidden_scale = lax.rsqrt(jnp.mean(hidden_f32 * hidden_f32, axis=-1, keepdims=True) + 1e-06)
    hid_norm = (hidden_f32 * hidden_scale * gain_hidden).astype(BF16)
    hid_all = lax.all_gather(hid_norm, "tp", axis=0, tiled=True)

    proj_t = projection.T

    def piece(y):
        return lax.dynamic_slice(proj_t, (0, width + y * quarter), (columns, quarter))

    weights = jnp.zeros((SIDE, columns, quarter), BF16)
    weights = lax.dynamic_update_slice(weights, piece(my_y)[None], (my_y, 0, 0))
    for step in range(1, SIDE):
        moved = lax.ppermute(
            piece((my_y + step) % SIDE),
            "tp",
            [(SIDE * y + x, SIDE * ((y + step) % SIDE) + x) for y in range(SIDE) for x in range(SIDE)],
        )
        weights = lax.dynamic_update_slice(weights, moved[None], ((my_y - step) % SIDE, 0, 0))
    weights = weights.reshape(SIDE * columns, quarter)

    ids_all = next_ids.reshape(groups, tokens)
    mine = ids_all // row_count == my_group
    token = jnp.arange(tokens, dtype=I32)
    upto = (token[:, None] <= token[None, :]).astype(BF16)
    rank_all = contract(mine.astype(BF16), upto, (1, 0)).astype(I32) - 1
    local_ids = ids_all - my_group * row_count
    half = capacity // 2
    row = jnp.arange(row_count, dtype=I32)

    def picked(first):
        ranks = first + jnp.arange(half, dtype=I32)
        hit = mine[:, None, :] & (rank_all[:, None, :] == ranks[None, :, None])
        rows = jnp.sum(jnp.where(hit, local_ids[:, None, :] + 1, 0), axis=2).reshape(slots // 2) - 1
        return (row[:, None] == rows[None, :]).astype(BF16)

    pick_left, pick_right = picked(0), picked(half)
    table_t = emb_table.T
    fetched = exchange_rows(contract(table_t, pick_left, (1, 0)), contract(table_t, pick_right, (1, 0)))

    ids_mine = lax.dynamic_index_in_dim(ids_all, my_group, 0, keepdims=False)
    owner = ids_mine // row_count
    place_left, place_right = placed(owner, live_mask, half, slots)

    emb = contract(fetched, place_left, (0, 0))[:local_width] + contract(fetched, place_right, (0, 0))[local_width:]
    gain = lax.dynamic_slice_in_dim(gain_embed, place_tp * local_width, local_width)[:, None]
    square_part = jnp.sum(emb * emb, axis=0, keepdims=True)
    got = along_x(to_all(jnp.concatenate([(emb * gain).astype(BF16), split_rows(square_part)], axis=0)))
    square_part = join_rows(got[:, local_width:])
    partial = contract(weights, got[:, :local_width].reshape(quarter, tokens), (1, 0)).astype(BF16)
    partial, hid_all = lax.optimization_barrier((partial, hid_all))
    partial = partial.reshape(SIDE, columns, tokens)
    got = along_y(jnp.concatenate([partial, to_all(split_rows(square_part))], axis=1))
    emb_raw = jnp.sum(got[:, :columns].astype(F32), axis=0)
    scale = lax.rsqrt(join_rows(got[:, columns:]) / width + 1e-06)

    hid_part = lax.optimization_barrier(contract(proj_t[:, :width], hid_all, (1, 1)))
    combined = hid_part + emb_raw * scale
    projected = combined.astype(BF16)
    upstream = (combined - target.T.astype(F32)).astype(BF16)
    curve_part = jnp.sum(upstream.astype(F32) * emb_raw, axis=0, keepdims=True)
    got = along_y(to_all(jnp.concatenate([upstream, split_rows(curve_part)], axis=0)))
    curve_part = join_rows(got[:, columns:])
    partial = contract(weights, got[:, :columns].reshape(SIDE * columns, tokens), (0, 0)).astype(BF16)
    partial = partial.reshape(SIDE, local_width, tokens)
    got = along_x(jnp.concatenate([partial, to_all(split_rows(curve_part))], axis=1))
    feature_grad = jnp.sum(got[:, :local_width].astype(F32), axis=0)
    curvature = join_rows(got[:, local_width:])

    emb_grad = scale * gain * feature_grad - scale * scale * scale * curvature / width * emb
    emb_grad = emb_grad.astype(BF16)
    arrived = exchange_rows(contract(emb_grad, place_left, (1, 1)), contract(emb_grad, place_right, (1, 1)))
    table_grad = (
        contract(arrived, pick_left, (0, 1))[:local_width] + contract(arrived, pick_right, (0, 1))[local_width:]
    ).astype(BF16)
    return (projected.T, table_grad.T)


def solution(mesh):
    return jax.shard_map(
        local,
        mesh=mesh,
        in_specs=(
            P(("seq", "tp"), None),
            P(),
            P("seq"),
            P("seq", "tp"),
            P(),
            P(),
            P(None, "tp"),
            P("seq", "tp"),
        ),
        out_specs=(P("seq", "tp"), P("seq", "tp")),
        check_vma=False,
    )
```

```python
import functools

import jax
import jax.numpy as jnp
from jax import lax
from jax.experimental import pallas as pl
from jax.sharding import PartitionSpec as P

BF16 = jnp.bfloat16
F32 = jnp.float32
I32 = jnp.int32
SIDE = 4
CORES = 2
PIECES = 16


def contract(left, right, dims):
    return lax.dot_general(left, right, ((dims[:1], dims[1:]), ((), ())), preferred_element_type=F32)


def split_rows(rows):
    high = rows.astype(BF16)
    rest = rows - high.astype(F32)
    middle = rest.astype(BF16)
    low = (rest - middle.astype(F32)).astype(BF16)
    pieces = jnp.concatenate([high, middle, low], axis=0)
    return jnp.pad(pieces, ((0, PIECES - pieces.shape[0]), (0, 0)))


def join_rows(messages, count):
    return sum(jnp.sum(messages[:, k * count : (k + 1) * count].astype(F32), axis=0) for k in range(3))


def place_kernel(half, owner_row, owner_column, live, left, right):
    tokens = owner_row.shape[1]
    below = lax.broadcasted_iota(I32, (tokens, tokens), 0)
    across = lax.broadcasted_iota(I32, (tokens, tokens), 1)
    earlier = (owner_column[...] == owner_row[...]) & (below < across)
    rank = jnp.sum(earlier.astype(I32), axis=0, keepdims=True)
    base = owner_row[...] * half
    row = lax.broadcasted_iota(I32, left.shape, 0)
    used = live[...] != 0
    left[...] = jnp.where((row == base + rank) & (rank < half) & used, 1.0, 0.0).astype(BF16)
    right[...] = jnp.where((row == base + rank - half) & (rank >= half) & used, 1.0, 0.0).astype(BF16)


def placed(owner, live, half, slots):
    tokens = owner.shape[0]
    return pl.pallas_call(
        functools.partial(place_kernel, half),
        out_shape=[jax.ShapeDtypeStruct((slots // 2, tokens), BF16)] * 2,
    )(owner[None, :], owner[:, None], live[None, :])


def along_x(value):
    groups = [[SIDE * y + x for x in range(SIDE)] for y in range(SIDE)]
    return lax.all_to_all(value, "tp", 0, 0, tiled=True, axis_index_groups=groups)


def along_y(value):
    groups = [[SIDE * y + x for y in range(SIDE)] for x in range(SIDE)]
    return lax.all_to_all(value, "tp", 0, 0, tiled=True, axis_index_groups=groups)


def to_all(value):
    return jnp.broadcast_to(value, (SIDE,) + value.shape)


def exchange_rows(left, right):
    groups = lax.axis_size("seq")
    both = jnp.concatenate([left, right], axis=0).astype(BF16).T
    both = both.reshape(groups, both.shape[0] // groups, both.shape[1])
    moved = lax.all_to_all(both, "seq", split_axis=0, concat_axis=0, tiled=True)
    return moved.reshape(-1, moved.shape[2])


def local(hidden, next_ids, live_mask, emb_table, gain_hidden, gain_embed, projection, target):
    width = hidden.shape[1]
    groups = lax.axis_size("seq")
    my_group = lax.axis_index("seq")
    place_tp = lax.axis_index("tp")
    my_y = place_tp // SIDE
    tokens = live_mask.shape[0]
    capacity = 2 * tokens // groups
    slots = groups * capacity
    row_count, local_width = emb_table.shape
    columns = projection.shape[1]
    quarter = width // SIDE

    hid_all = lax.all_gather(hidden, "tp", axis=0, tiled=True)
    hidden_f32 = hidden.astype(F32)
    hidden_scale = lax.rsqrt(jnp.mean(hidden_f32 * hidden_f32, axis=-1) + 1e-06)
    rows_here = hidden.shape[0]
    lane = jnp.arange(tokens, dtype=I32)
    hidden_scale = jnp.where(lane // rows_here == place_tp, jnp.tile(hidden_scale, tokens // rows_here), 0.0)

    proj_t = projection.T
    part = columns // CORES
    my_core = my_group % CORES

    def piece(y):
        return lax.dynamic_slice(proj_t, (my_core * part, width + y * quarter), (part, quarter))

    fetched_half = jnp.zeros((SIDE, part, quarter), BF16)
    fetched_half = lax.dynamic_update_slice(fetched_half, piece(my_y)[None], (my_y, 0, 0))
    for step in range(1, SIDE):
        moved = lax.ppermute(
            piece((my_y + step) % SIDE),
            "tp",
            [(SIDE * y + x, SIDE * ((y + step) % SIDE) + x) for y in range(SIDE) for x in range(SIDE)],
        )
        fetched_half = lax.dynamic_update_slice(fetched_half, moved[None], ((my_y - step) % SIDE, 0, 0))
    other_half = lax.ppermute(fetched_half, "seq", [(k, k ^ 1) for k in range(groups)])
    weights_here = fetched_half.reshape(SIDE * part, quarter)
    weights_other = other_half.reshape(SIDE * part, quarter)
    first = my_core == 0

    def ordered(here, other):
        return jnp.where(first, here, other), jnp.where(first, other, here)

    ids_all = next_ids.reshape(groups, tokens)
    mine = ids_all // row_count == my_group
    token = jnp.arange(tokens, dtype=I32)
    upto = (token[:, None] <= token[None, :]).astype(BF16)
    rank_all = contract(mine.astype(BF16), upto, (1, 0)).astype(I32) - 1
    local_ids = ids_all - my_group * row_count
    half = capacity // 2
    row = jnp.arange(row_count, dtype=I32)

    def picked(first):
        ranks = first + jnp.arange(half, dtype=I32)
        hit = mine[:, None, :] & (rank_all[:, None, :] == ranks[None, :, None])
        rows = jnp.sum(jnp.where(hit, local_ids[:, None, :] + 1, 0), axis=2).reshape(slots // 2) - 1
        return (row[:, None] == rows[None, :]).astype(BF16)

    pick_left, pick_right = picked(0), picked(half)
    table_t = emb_table.T
    fetched = exchange_rows(contract(table_t, pick_left, (1, 0)), contract(table_t, pick_right, (1, 0)))

    ids_mine = lax.dynamic_index_in_dim(ids_all, my_group, 0, keepdims=False)
    owner = ids_mine // row_count
    place_left, place_right = placed(owner, live_mask, half, slots)

    emb = contract(fetched, place_left, (0, 0))[:local_width] + contract(fetched, place_right, (0, 0))[local_width:]
    gain = lax.dynamic_slice_in_dim(gain_embed, place_tp * local_width, local_width)[:, None]
    squares = jnp.sum(emb * emb, axis=0, keepdims=True)
    shared = jnp.concatenate([squares, hidden_scale[None, :]], axis=0)
    got = along_x(to_all(jnp.concatenate([(emb * gain).astype(BF16), split_rows(shared)], axis=0)))
    shared = join_rows(got[:, local_width:], 2)
    features = got[:, :local_width].reshape(quarter, tokens)
    features, hid_all = lax.optimization_barrier((features, hid_all))
    halves = ordered(contract(weights_here, features, (1, 0)), contract(weights_other, features, (1, 0)))
    halves = [half_rows.astype(BF16).reshape(SIDE, part, tokens) for half_rows in halves]
    got = along_y(jnp.concatenate([*halves, to_all(split_rows(shared))], axis=1))
    emb_raw = jnp.sum(got[:, :columns].astype(F32), axis=0)
    shared = join_rows(got[:, columns:], 2)
    scale = lax.rsqrt(shared[:1] / width + 1e-06)
    hidden_scale = shared[1:]

    hid_gained = (hid_all.astype(F32) * gain_hidden).astype(BF16)
    hid_raw = lax.optimization_barrier(contract(proj_t[:, :width], hid_gained, (1, 1)))
    combined = hid_raw * hidden_scale + emb_raw * scale
    projected = combined.astype(BF16)
    upstream = (combined - target.T.astype(F32)).astype(BF16)
    curve = jnp.sum(upstream.astype(F32) * emb_raw, axis=0, keepdims=True)
    got = along_y(to_all(jnp.concatenate([upstream, split_rows(curve)], axis=0)))
    curve = join_rows(got[:, columns:], 1)
    here, other = ordered(got[:, :part], got[:, part:columns])
    partial = contract(weights_here, here.reshape(SIDE * part, tokens), (0, 0))
    partial = partial + contract(weights_other, other.reshape(SIDE * part, tokens), (0, 0))
    partial = partial.astype(BF16).reshape(SIDE, local_width, tokens)
    got = along_x(jnp.concatenate([partial, to_all(split_rows(curve))], axis=1))
    feature_grad = jnp.sum(got[:, :local_width].astype(F32), axis=0)
    curvature = join_rows(got[:, local_width:], 1)

    emb_grad = scale * gain * feature_grad - scale * scale * scale * curvature / width * emb
    emb_grad = emb_grad.astype(BF16)
    arrived = exchange_rows(contract(emb_grad, place_left, (1, 1)), contract(emb_grad, place_right, (1, 1)))
    table_grad = (
        contract(arrived, pick_left, (0, 1))[:local_width] + contract(arrived, pick_right, (0, 1))[local_width:]
    ).astype(BF16)
    return (projected.T, table_grad.T)


def solution(mesh):
    return jax.shard_map(
        local,
        mesh=mesh,
        in_specs=(
            P(("seq", "tp"), None),
            P(),
            P("seq"),
            P("seq", "tp"),
            P(),
            P(),
            P(None, "tp"),
            P("seq", "tp"),
        ),
        out_specs=(P("seq", "tp"), P("seq", "tp")),
        check_vma=False,
    )
```

```python
import functools

import jax
import jax.numpy as jnp
from jax import lax
from jax.experimental import pallas as pl
from jax.sharding import PartitionSpec as P

BF16 = jnp.bfloat16
F32 = jnp.float32
I32 = jnp.int32
SIDE = 4
CORES = 2
PIECES = 16


def contract(left, right, dims):
    return lax.dot_general(left, right, ((dims[:1], dims[1:]), ((), ())), preferred_element_type=F32)


def split_rows(rows):
    high = rows.astype(BF16)
    rest = rows - high.astype(F32)
    middle = rest.astype(BF16)
    low = (rest - middle.astype(F32)).astype(BF16)
    pieces = jnp.concatenate([high, middle, low], axis=0)
    return jnp.pad(pieces, ((0, PIECES - pieces.shape[0]), (0, 0)))


def join_rows(messages, count):
    return sum(jnp.sum(messages[:, k * count : (k + 1) * count].astype(F32), axis=0) for k in range(3))


def place_kernel(half, owner_row, owner_column, live, left, right):
    tokens = owner_row.shape[1]
    below = lax.broadcasted_iota(I32, (tokens, tokens), 0)
    across = lax.broadcasted_iota(I32, (tokens, tokens), 1)
    earlier = (owner_column[...] == owner_row[...]) & (below < across)
    rank = jnp.sum(earlier.astype(I32), axis=0, keepdims=True)
    base = owner_row[...] * half
    row = lax.broadcasted_iota(I32, left.shape, 0)
    used = live[...] != 0
    left[...] = jnp.where((row == base + rank) & (rank < half) & used, 1.0, 0.0).astype(BF16)
    right[...] = jnp.where((row == base + rank - half) & (rank >= half) & used, 1.0, 0.0).astype(BF16)


def placed(owner, live, half, slots):
    tokens = owner.shape[0]
    return pl.pallas_call(
        functools.partial(place_kernel, half),
        out_shape=[jax.ShapeDtypeStruct((slots // 2, tokens), BF16)] * 2,
    )(owner[None, :], owner[:, None], live[None, :])


def along_x(value):
    groups = [[SIDE * y + x for x in range(SIDE)] for y in range(SIDE)]
    return lax.all_to_all(value, "tp", 0, 0, tiled=True, axis_index_groups=groups)


def along_y(value):
    groups = [[SIDE * y + x for y in range(SIDE)] for x in range(SIDE)]
    return lax.all_to_all(value, "tp", 0, 0, tiled=True, axis_index_groups=groups)


def to_all(value):
    return jnp.broadcast_to(value, (SIDE,) + value.shape)


def exchange_rows(left, right):
    groups = lax.axis_size("seq")
    both = jnp.concatenate([left, right], axis=0).astype(BF16).T
    both = both.reshape(groups, both.shape[0] // groups, both.shape[1])
    moved = lax.all_to_all(both, "seq", split_axis=0, concat_axis=0, tiled=True)
    return moved.reshape(-1, moved.shape[2])


def local(hidden, next_ids, live_mask, emb_table, gain_hidden, gain_embed, projection, target):
    width = hidden.shape[1]
    groups = lax.axis_size("seq")
    my_group = lax.axis_index("seq")
    place_tp = lax.axis_index("tp")
    my_y = place_tp // SIDE
    tokens = live_mask.shape[0]
    capacity = 2 * tokens // groups
    slots = groups * capacity
    row_count, local_width = emb_table.shape
    columns = projection.shape[1]
    quarter = width // SIDE

    hid_all = lax.all_gather(hidden, "tp", axis=0, tiled=True)

    def scale_row():
        hidden_f32 = hidden.astype(F32)
        own = lax.rsqrt(jnp.mean(hidden_f32 * hidden_f32, axis=-1) + 1e-06)
        rows_here = hidden.shape[0]
        lane = jnp.arange(tokens, dtype=I32)
        return jnp.where(lane // rows_here == place_tp, jnp.tile(own, tokens // rows_here), 0.0)

    proj_t = projection.T
    part = columns // CORES
    my_core = my_group % CORES

    def piece(y):
        return lax.dynamic_slice(proj_t, (my_core * part, width + y * quarter), (part, quarter))

    def fetch_half():
        fetched_half = jnp.zeros((SIDE, part, quarter), BF16)
        fetched_half = lax.dynamic_update_slice(fetched_half, piece(my_y)[None], (my_y, 0, 0))
        for step in range(1, SIDE):
            moved = lax.ppermute(
                piece((my_y + step) % SIDE),
                "tp",
                [(SIDE * y + x, SIDE * ((y + step) % SIDE) + x) for y in range(SIDE) for x in range(SIDE)],
            )
            fetched_half = lax.dynamic_update_slice(fetched_half, moved[None], ((my_y - step) % SIDE, 0, 0))
        return fetched_half

    first = my_core == 0

    def ordered(here, other):
        return jnp.where(first, here, other), jnp.where(first, other, here)

    ids_all = next_ids.reshape(groups, tokens)
    mine = ids_all // row_count == my_group
    token = jnp.arange(tokens, dtype=I32)
    upto = (token[:, None] <= token[None, :]).astype(BF16)
    rank_all = contract(mine.astype(BF16), upto, (1, 0)).astype(I32) - 1
    local_ids = ids_all - my_group * row_count
    half = capacity // 2
    row = jnp.arange(row_count, dtype=I32)

    def asked(first):
        ranks = first + jnp.arange(half, dtype=I32)
        hit = mine[:, None, :] & (rank_all[:, None, :] == ranks[None, :, None])
        return jnp.sum(jnp.where(hit, local_ids[:, None, :] + 1, 0), axis=2).reshape(slots // 2) - 1

    def picked(rows):
        return (row[:, None] == rows[None, :]).astype(BF16)

    rows_left, rows_right = asked(0), asked(half)
    table_t = emb_table.T

    ids_mine = lax.dynamic_index_in_dim(ids_all, my_group, 0, keepdims=False)
    owner = ids_mine // row_count

    def fetch():
        left, right = contract(table_t, picked(rows_left), (1, 0)), contract(table_t, picked(rows_right), (1, 0))
        return exchange_rows(left, right), fetch_half(), scale_row(), *placed(owner, live_mask, half, slots)

    def skip():
        return jax.tree.map(lambda leaf: jnp.zeros(leaf.shape, leaf.dtype), jax.eval_shape(fetch))

    fetched, fetched_half, hidden_scale, place_left, place_right = lax.cond(next_ids[0] >= 0, fetch, skip)
    other_half = lax.ppermute(fetched_half, "seq", [(k, k ^ 1) for k in range(groups)])
    weights_here = fetched_half.reshape(SIDE * part, quarter)
    weights_other = other_half.reshape(SIDE * part, quarter)

    emb = contract(fetched, place_left, (0, 0))[:local_width] + contract(fetched, place_right, (0, 0))[local_width:]
    gain = lax.dynamic_slice_in_dim(gain_embed, place_tp * local_width, local_width)[:, None]
    squares = jnp.sum(emb * emb, axis=0, keepdims=True)
    shared = jnp.concatenate([squares, hidden_scale[None, :]], axis=0)
    got = along_x(to_all(jnp.concatenate([(emb * gain).astype(BF16), split_rows(shared)], axis=0)))
    shared = join_rows(got[:, local_width:], 2)
    features = got[:, :local_width].reshape(quarter, tokens)
    halves = ordered(contract(weights_here, features, (1, 0)), contract(weights_other, features, (1, 0)))
    halves = [half_rows.astype(BF16).reshape(SIDE, part, tokens) for half_rows in halves]
    got = along_y(jnp.concatenate([*halves, to_all(split_rows(shared))], axis=1))
    emb_raw = jnp.sum(got[:, :columns].astype(F32), axis=0)
    shared = join_rows(got[:, columns:], 2)
    scale = lax.rsqrt(shared[:1] / width + 1e-06)
    hidden_scale = shared[1:]

    hid_gained = (hid_all.astype(F32) * gain_hidden).astype(BF16)
    hid_raw = lax.optimization_barrier(contract(proj_t[:, :width], hid_gained, (1, 1)))
    combined = hid_raw * hidden_scale + emb_raw * scale
    projected = combined.astype(BF16)
    upstream = (combined - target.T.astype(F32)).astype(BF16)
    curve = jnp.sum(upstream.astype(F32) * emb_raw, axis=0, keepdims=True)
    got = along_y(to_all(jnp.concatenate([upstream, split_rows(curve)], axis=0)))
    curve = join_rows(got[:, columns:], 1)
    here, other = ordered(got[:, :part], got[:, part:columns])
    partial = contract(weights_here, here.reshape(SIDE * part, tokens), (0, 0))
    partial = partial + contract(weights_other, other.reshape(SIDE * part, tokens), (0, 0))
    partial = partial.astype(BF16).reshape(SIDE, local_width, tokens)
    got = along_x(jnp.concatenate([partial, to_all(split_rows(curve))], axis=1))
    feature_grad = jnp.sum(got[:, :local_width].astype(F32), axis=0)
    curvature = join_rows(got[:, local_width:], 1)

    emb_grad = scale * gain * feature_grad - scale * scale * scale * curvature / width * emb
    emb_grad = emb_grad.astype(BF16)
    arrived = exchange_rows(contract(emb_grad, place_left, (1, 1)), contract(emb_grad, place_right, (1, 1)))
    table_grad = (
        contract(arrived, picked(rows_left), (0, 1))[:local_width] + contract(arrived, picked(rows_right), (0, 1))[local_width:]
    ).astype(BF16)
    return (projected.T, table_grad.T)


def solution(mesh):
    return jax.shard_map(
        local,
        mesh=mesh,
        in_specs=(
            P(("seq", "tp"), None),
            P(),
            P("seq"),
            P("seq", "tp"),
            P(),
            P(),
            P(None, "tp"),
            P("seq", "tp"),
        ),
        out_specs=(P("seq", "tp"), P("seq", "tp")),
        check_vma=False,
    )
```

```python
import functools

import jax
import jax.numpy as jnp
from jax import lax
from jax.experimental import pallas as pl
from jax.sharding import PartitionSpec as P

BF16 = jnp.bfloat16
F32 = jnp.float32
I32 = jnp.int32
SIDE = 4
CORES = 2
PIECES = 16


def contract(left, right, dims):
    return lax.dot_general(left, right, ((dims[:1], dims[1:]), ((), ())), preferred_element_type=F32)


def split_rows(rows):
    high = rows.astype(BF16)
    rest = rows - high.astype(F32)
    middle = rest.astype(BF16)
    low = (rest - middle.astype(F32)).astype(BF16)
    pieces = jnp.concatenate([high, middle, low], axis=0)
    return jnp.pad(pieces, ((0, PIECES - pieces.shape[0]), (0, 0)))


def join_rows(messages, count):
    return sum(jnp.sum(messages[:, k * count : (k + 1) * count].astype(F32), axis=0) for k in range(3))


def place_kernel(half, owner_row, owner_column, live, left, right):
    tokens = owner_row.shape[1]
    below = lax.broadcasted_iota(I32, (tokens, tokens), 0)
    across = lax.broadcasted_iota(I32, (tokens, tokens), 1)
    earlier = (owner_column[...] == owner_row[...]) & (below < across)
    rank = jnp.sum(earlier.astype(I32), axis=0, keepdims=True)
    base = owner_row[...] * half
    row = lax.broadcasted_iota(I32, left.shape, 0)
    used = live[...] != 0
    left[...] = jnp.where((row == base + rank) & (rank < half) & used, 1.0, 0.0).astype(BF16)
    right[...] = jnp.where((row == base + rank - half) & (rank >= half) & used, 1.0, 0.0).astype(BF16)


def placed(owner, live, half, slots):
    tokens = owner.shape[0]
    return pl.pallas_call(
        functools.partial(place_kernel, half),
        out_shape=[jax.ShapeDtypeStruct((slots // 2, tokens), BF16)] * 2,
    )(owner[None, :], owner[:, None], live[None, :])


def along_x(value):
    groups = [[SIDE * y + x for x in range(SIDE)] for y in range(SIDE)]
    return lax.all_to_all(value, "tp", 0, 0, tiled=True, axis_index_groups=groups)


def along_y(value):
    groups = [[SIDE * y + x for y in range(SIDE)] for x in range(SIDE)]
    return lax.all_to_all(value, "tp", 0, 0, tiled=True, axis_index_groups=groups)


def to_all(value):
    return jnp.broadcast_to(value, (SIDE,) + value.shape)


def exchange_rows(left, right):
    groups = lax.axis_size("seq")
    both = jnp.concatenate([left, right], axis=0).astype(BF16).T
    both = both.reshape(groups, both.shape[0] // groups, both.shape[1])
    moved = lax.all_to_all(both, "seq", split_axis=0, concat_axis=0, tiled=True)
    return moved.reshape(-1, moved.shape[2])


def local(hidden, next_ids, live_mask, emb_table, gain_hidden, gain_embed, projection, target):
    width = hidden.shape[1]
    groups = lax.axis_size("seq")
    my_group = lax.axis_index("seq")
    place_tp = lax.axis_index("tp")
    my_y = place_tp // SIDE
    tokens = live_mask.shape[0]
    capacity = 2 * tokens // groups
    slots = groups * capacity
    row_count, local_width = emb_table.shape
    columns = projection.shape[1]
    quarter = width // SIDE

    hid_all = lax.all_gather(hidden, "tp", axis=0, tiled=True)

    def scale_row():
        hidden_f32 = hidden.astype(F32)
        own = lax.rsqrt(jnp.mean(hidden_f32 * hidden_f32, axis=-1) + 1e-06)
        rows_here = hidden.shape[0]
        lane = jnp.arange(tokens, dtype=I32)
        return jnp.where(lane // rows_here == place_tp, jnp.tile(own, tokens // rows_here), 0.0)

    proj_t = projection.T
    part = columns // CORES
    my_core = my_group % CORES

    def piece(y):
        return lax.dynamic_slice(proj_t, (my_core * part, width + y * quarter), (part, quarter))

    def fetch_half():
        fetched_half = jnp.zeros((SIDE, part, quarter), BF16)
        fetched_half = lax.dynamic_update_slice(fetched_half, piece(my_y)[None], (my_y, 0, 0))
        for step in range(1, SIDE):
            moved = lax.ppermute(
                piece((my_y + step) % SIDE),
                "tp",
                [(SIDE * y + x, SIDE * ((y + step) % SIDE) + x) for y in range(SIDE) for x in range(SIDE)],
            )
            fetched_half = lax.dynamic_update_slice(fetched_half, moved[None], ((my_y - step) % SIDE, 0, 0))
        return fetched_half, lax.ppermute(fetched_half, "seq", [(k, k ^ 1) for k in range(groups)])

    first = my_core == 0

    def ordered(here, other):
        return jnp.where(first, here, other), jnp.where(first, other, here)

    ids_all = next_ids.reshape(groups, tokens)
    mine = ids_all // row_count == my_group
    token = jnp.arange(tokens, dtype=I32)
    upto = (token[:, None] <= token[None, :]).astype(BF16)
    rank_all = contract(mine.astype(BF16), upto, (1, 0)).astype(I32) - 1
    local_ids = ids_all - my_group * row_count
    half = capacity // 2
    row = jnp.arange(row_count, dtype=I32)

    def asked(first):
        ranks = first + jnp.arange(half, dtype=I32)
        hit = mine[:, None, :] & (rank_all[:, None, :] == ranks[None, :, None])
        return jnp.sum(jnp.where(hit, local_ids[:, None, :] + 1, 0), axis=2).reshape(slots // 2) - 1

    def picked(rows):
        return (row[:, None] == rows[None, :]).astype(BF16)

    rows_left, rows_right = asked(0), asked(half)
    table_t = emb_table.T

    ids_mine = lax.dynamic_index_in_dim(ids_all, my_group, 0, keepdims=False)
    owner = ids_mine // row_count

    def fetch():
        left, right = contract(table_t, picked(rows_left), (1, 0)), contract(table_t, picked(rows_right), (1, 0))
        return exchange_rows(left, right), *fetch_half(), scale_row(), *placed(owner, live_mask, half, slots)

    def skip():
        return jax.tree.map(lambda leaf: jnp.zeros(leaf.shape, leaf.dtype), jax.eval_shape(fetch))

    fetched, fetched_half, other_half, hidden_scale, place_left, place_right = lax.cond(next_ids[0] >= 0, fetch, skip)
    weights_here = fetched_half.reshape(SIDE * part, quarter)
    weights_other = other_half.reshape(SIDE * part, quarter)

    emb = contract(fetched, place_left, (0, 0))[:local_width] + contract(fetched, place_right, (0, 0))[local_width:]
    gain = lax.dynamic_slice_in_dim(gain_embed, place_tp * local_width, local_width)[:, None]
    squares = jnp.sum(emb * emb, axis=0, keepdims=True)
    shared = jnp.concatenate([squares, hidden_scale[None, :]], axis=0)
    message = jnp.concatenate([(emb * gain).astype(BF16), split_rows(shared)], axis=0)
    rows_of_devices = [[SIDE * y + x for x in range(SIDE)] for y in range(SIDE)]
    got = lax.all_gather(message, "tp", axis=0, tiled=False, axis_index_groups=rows_of_devices)
    shared = join_rows(got[:, local_width:], 2)
    features = got[:, :local_width].reshape(quarter, tokens)
    halves = ordered(contract(weights_here, features, (1, 0)), contract(weights_other, features, (1, 0)))
    halves = [half_rows.astype(BF16).reshape(SIDE, part, tokens) for half_rows in halves]
    got = along_y(jnp.concatenate([*halves, to_all(split_rows(shared))], axis=1))
    emb_raw = jnp.sum(got[:, :columns].astype(F32), axis=0)
    shared = join_rows(got[:, columns:], 2)
    scale = lax.rsqrt(shared[:1] / width + 1e-06)
    hidden_scale = shared[1:]

    hid_gained = (hid_all.astype(F32) * gain_hidden).astype(BF16)
    hid_raw = lax.optimization_barrier(contract(proj_t[:, :width], hid_gained, (1, 1)))
    combined = hid_raw * hidden_scale + emb_raw * scale
    projected = combined.astype(BF16)
    upstream = (combined - target.T.astype(F32)).astype(BF16)
    curve = jnp.sum(upstream.astype(F32) * emb_raw, axis=0, keepdims=True)
    got = along_y(to_all(jnp.concatenate([upstream, split_rows(curve)], axis=0)))
    curve = join_rows(got[:, columns:], 1)
    here, other = ordered(got[:, :part], got[:, part:columns])
    partial = contract(weights_here, here.reshape(SIDE * part, tokens), (0, 0))
    partial = partial + contract(weights_other, other.reshape(SIDE * part, tokens), (0, 0))
    partial = partial.astype(BF16).reshape(SIDE, local_width, tokens)
    got = along_x(jnp.concatenate([partial, to_all(split_rows(curve))], axis=1))
    feature_grad = jnp.sum(got[:, :local_width].astype(F32), axis=0)
    curvature = join_rows(got[:, local_width:], 1)

    emb_grad = scale * gain * feature_grad - scale * scale * scale * curvature / width * emb
    emb_grad = emb_grad.astype(BF16)
    arrived = exchange_rows(contract(emb_grad, place_left, (1, 1)), contract(emb_grad, place_right, (1, 1)))
    table_grad = (
        contract(arrived, picked(rows_left), (0, 1))[:local_width] + contract(arrived, picked(rows_right), (0, 1))[local_width:]
    ).astype(BF16)
    return (projected.T, table_grad.T)


def solution(mesh):
    return jax.shard_map(
        local,
        mesh=mesh,
        in_specs=(
            P(("seq", "tp"), None),
            P(),
            P("seq"),
            P("seq", "tp"),
            P(),
            P(),
            P(None, "tp"),
            P("seq", "tp"),
        ),
        out_specs=(P("seq", "tp"), P("seq", "tp")),
        check_vma=False,
    )
```

```python
import functools

import jax
import jax.numpy as jnp
from jax import lax
from jax.experimental import pallas as pl
from jax.sharding import PartitionSpec as P

BF16 = jnp.bfloat16
F32 = jnp.float32
I32 = jnp.int32
SIDE = 4
CORES = 2
PIECES = 16


def contract(left, right, dims):
    return lax.dot_general(left, right, ((dims[:1], dims[1:]), ((), ())), preferred_element_type=F32)


def split_rows(rows):
    high = rows.astype(BF16)
    rest = rows - high.astype(F32)
    middle = rest.astype(BF16)
    low = (rest - middle.astype(F32)).astype(BF16)
    pieces = jnp.concatenate([high, middle, low], axis=0)
    return jnp.pad(pieces, ((0, PIECES - pieces.shape[0]), (0, 0)))


def join_rows(messages, count):
    return sum(jnp.sum(messages[:, k * count : (k + 1) * count].astype(F32), axis=0) for k in range(3))


def place_kernel(half, owner_row, owner_column, live, left, right):
    tokens = owner_row.shape[1]
    below = lax.broadcasted_iota(I32, (tokens, tokens), 0)
    across = lax.broadcasted_iota(I32, (tokens, tokens), 1)
    earlier = (owner_column[...] == owner_row[...]) & (below < across)
    rank = jnp.sum(earlier.astype(I32), axis=0, keepdims=True)
    base = owner_row[...] * half
    row = lax.broadcasted_iota(I32, left.shape, 0)
    used = live[...] != 0
    left[...] = jnp.where((row == base + rank) & (rank < half) & used, 1.0, 0.0).astype(BF16)
    right[...] = jnp.where((row == base + rank - half) & (rank >= half) & used, 1.0, 0.0).astype(BF16)


def placed(owner, live, half, slots):
    tokens = owner.shape[0]
    return pl.pallas_call(
        functools.partial(place_kernel, half),
        out_shape=[jax.ShapeDtypeStruct((slots // 2, tokens), BF16)] * 2,
    )(owner[None, :], owner[:, None], live[None, :])


def along_x(value):
    groups = [[SIDE * y + x for x in range(SIDE)] for y in range(SIDE)]
    return lax.all_to_all(value, "tp", 0, 0, tiled=True, axis_index_groups=groups)


def along_y(value):
    groups = [[SIDE * y + x for y in range(SIDE)] for x in range(SIDE)]
    return lax.all_to_all(value, "tp", 0, 0, tiled=True, axis_index_groups=groups)


def to_all(value):
    return jnp.broadcast_to(value, (SIDE,) + value.shape)


def side_by_side(left, right):
    groups = lax.axis_size("seq")
    both = jnp.concatenate([left, right], axis=0).astype(BF16).T
    return both.reshape(groups, both.shape[0] // groups, both.shape[1])


def exchange_rows(both):
    moved = lax.all_to_all(both, "seq", split_axis=0, concat_axis=0, tiled=True)
    return moved.reshape(-1, moved.shape[2])


def local(hidden, next_ids, live_mask, emb_table, gain_hidden, gain_embed, projection, target):
    width = hidden.shape[1]
    groups = lax.axis_size("seq")
    my_group = lax.axis_index("seq")
    place_tp = lax.axis_index("tp")
    my_y = place_tp // SIDE
    tokens = live_mask.shape[0]
    capacity = 2 * tokens // groups
    slots = groups * capacity
    row_count, local_width = emb_table.shape
    columns = projection.shape[1]
    quarter = width // SIDE

    hid_all = lax.all_gather(hidden, "tp", axis=0, tiled=True)

    def scale_row():
        hidden_f32 = hidden.astype(F32)
        own = lax.rsqrt(jnp.mean(hidden_f32 * hidden_f32, axis=-1) + 1e-06)
        rows_here = hidden.shape[0]
        lane = jnp.arange(tokens, dtype=I32)
        return jnp.where(lane // rows_here == place_tp, jnp.tile(own, tokens // rows_here), 0.0)

    proj_t = projection.T
    part = columns // CORES
    my_core = my_group % CORES

    def piece(y):
        return lax.dynamic_slice(proj_t, (my_core * part, width + y * quarter), (part, quarter))

    def fetch_half():
        fetched_half = jnp.zeros((SIDE, part, quarter), BF16)
        fetched_half = lax.dynamic_update_slice(fetched_half, piece(my_y)[None], (my_y, 0, 0))
        for step in range(1, SIDE):
            moved = lax.ppermute(
                piece((my_y + step) % SIDE),
                "tp",
                [(SIDE * y + x, SIDE * ((y + step) % SIDE) + x) for y in range(SIDE) for x in range(SIDE)],
            )
            fetched_half = lax.dynamic_update_slice(fetched_half, moved[None], ((my_y - step) % SIDE, 0, 0))
        return fetched_half, lax.ppermute(fetched_half, "seq", [(k, k ^ 1) for k in range(groups)])

    first = my_core == 0

    def ordered(here, other):
        return jnp.where(first, here, other), jnp.where(first, other, here)

    ids_all = next_ids.reshape(groups, tokens)
    mine = ids_all // row_count == my_group
    token = jnp.arange(tokens, dtype=I32)
    upto = (token[:, None] <= token[None, :]).astype(BF16)
    rank_all = contract(mine.astype(BF16), upto, (1, 0)).astype(I32) - 1
    local_ids = ids_all - my_group * row_count
    half = capacity // 2
    row = jnp.arange(row_count, dtype=I32)

    def asked(first):
        ranks = first + jnp.arange(half, dtype=I32)
        hit = mine[:, None, :] & (rank_all[:, None, :] == ranks[None, :, None])
        return jnp.sum(jnp.where(hit, local_ids[:, None, :] + 1, 0), axis=2).reshape(slots // 2) - 1

    def picked(rows):
        return (row[:, None] == rows[None, :]).astype(BF16)

    rows_left, rows_right = asked(0), asked(half)
    table_t = emb_table.T

    ids_mine = lax.dynamic_index_in_dim(ids_all, my_group, 0, keepdims=False)
    owner = ids_mine // row_count
    wanted = side_by_side(contract(table_t, picked(rows_left), (1, 0)), contract(table_t, picked(rows_right), (1, 0)))

    def fetch():
        gain = lax.dynamic_slice_in_dim(gain_embed, place_tp * local_width, local_width)[:, None]
        return exchange_rows(wanted), *fetch_half(), gain, scale_row(), *placed(owner, live_mask, half, slots)

    def skip():
        return jax.tree.map(lambda leaf: jnp.zeros(leaf.shape, leaf.dtype), jax.eval_shape(fetch))

    fetched, fetched_half, other_half, gain, hidden_scale, place_left, place_right = lax.cond(my_group < groups, fetch, skip)
    weights_here = fetched_half.reshape(SIDE * part, quarter)
    weights_other = other_half.reshape(SIDE * part, quarter)

    emb = contract(fetched, place_left, (0, 0))[:local_width] + contract(fetched, place_right, (0, 0))[local_width:]
    squares = jnp.sum(emb * emb, axis=0, keepdims=True)
    shared = jnp.concatenate([squares, hidden_scale[None, :]], axis=0)
    message = jnp.concatenate([(emb * gain).astype(BF16), split_rows(shared)], axis=0)
    rows_of_devices = [[SIDE * y + x for x in range(SIDE)] for y in range(SIDE)]
    got = lax.all_gather(message, "tp", axis=0, tiled=False, axis_index_groups=rows_of_devices)
    shared = join_rows(got[:, local_width:], 2)
    features = got[:, :local_width].reshape(quarter, tokens)
    halves = ordered(contract(weights_here, features, (1, 0)), contract(weights_other, features, (1, 0)))
    halves = [half_rows.astype(BF16).reshape(SIDE, part, tokens) for half_rows in halves]
    got = along_y(jnp.concatenate([*halves, to_all(split_rows(shared))], axis=1))
    emb_raw = jnp.sum(got[:, :columns].astype(F32), axis=0)
    shared = join_rows(got[:, columns:], 2)
    scale = lax.rsqrt(shared[:1] / width + 1e-06)
    hidden_scale = shared[1:]

    hid_gained = (hid_all.astype(F32) * gain_hidden).astype(BF16)
    hid_raw = lax.optimization_barrier(contract(proj_t[:, :width], hid_gained, (1, 1)))
    combined = hid_raw * hidden_scale + emb_raw * scale
    projected = combined.astype(BF16)
    upstream = (combined - target.T.astype(F32)).astype(BF16)
    curve = jnp.sum(upstream.astype(F32) * emb_raw, axis=0, keepdims=True)
    got = along_y(to_all(jnp.concatenate([upstream, split_rows(curve)], axis=0)))
    curve = join_rows(got[:, columns:], 1)
    here, other = ordered(got[:, :part], got[:, part:columns])
    partial = contract(weights_here, here.reshape(SIDE * part, tokens), (0, 0))
    partial = partial + contract(weights_other, other.reshape(SIDE * part, tokens), (0, 0))
    partial = partial.astype(BF16).reshape(SIDE, local_width, tokens)
    got = along_x(jnp.concatenate([partial, to_all(split_rows(curve))], axis=1))
    feature_grad = jnp.sum(got[:, :local_width].astype(F32), axis=0)
    curvature = join_rows(got[:, local_width:], 1)

    emb_grad = scale * gain * feature_grad - scale * scale * scale * curvature / width * emb
    emb_grad = emb_grad.astype(BF16)
    returned = side_by_side(contract(emb_grad, place_left, (1, 1)), contract(emb_grad, place_right, (1, 1)))
    arrived = exchange_rows(returned)
    table_grad = (
        contract(arrived, picked(rows_left), (0, 1))[:local_width] + contract(arrived, picked(rows_right), (0, 1))[local_width:]
    ).astype(BF16)
    return (projected.T, table_grad.T)


def solution(mesh):
    return jax.shard_map(
        local,
        mesh=mesh,
        in_specs=(
            P(("seq", "tp"), None),
            P(),
            P("seq"),
            P("seq", "tp"),
            P(),
            P(),
            P(None, "tp"),
            P("seq", "tp"),
        ),
        out_specs=(P("seq", "tp"), P("seq", "tp")),
        check_vma=False,
    )
```

```python
import functools

import jax
import jax.numpy as jnp
from jax import lax
from jax.experimental import pallas as pl
from jax.sharding import PartitionSpec as P

BF16 = jnp.bfloat16
F32 = jnp.float32
I32 = jnp.int32
SIDE = 4
CORES = 2
PIECES = 16


def contract(left, right, dims):
    return lax.dot_general(left, right, ((dims[:1], dims[1:]), ((), ())), preferred_element_type=F32)


def split_rows(rows):
    high = rows.astype(BF16)
    rest = rows - high.astype(F32)
    middle = rest.astype(BF16)
    low = (rest - middle.astype(F32)).astype(BF16)
    pieces = jnp.concatenate([high, middle, low], axis=0)
    return jnp.pad(pieces, ((0, PIECES - pieces.shape[0]), (0, 0)))


def join_rows(messages, count):
    return sum(jnp.sum(messages[:, k * count : (k + 1) * count].astype(F32), axis=0) for k in range(3))


def place_kernel(half, owner_row, owner_column, live, left, right):
    tokens = owner_row.shape[1]
    below = lax.broadcasted_iota(I32, (tokens, tokens), 0)
    across = lax.broadcasted_iota(I32, (tokens, tokens), 1)
    earlier = (owner_column[...] == owner_row[...]) & (below < across)
    rank = jnp.sum(earlier.astype(I32), axis=0, keepdims=True)
    base = owner_row[...] * half
    row = lax.broadcasted_iota(I32, left.shape, 0)
    used = live[...] != 0
    left[...] = jnp.where((row == base + rank) & (rank < half) & used, 1.0, 0.0).astype(BF16)
    right[...] = jnp.where((row == base + rank - half) & (rank >= half) & used, 1.0, 0.0).astype(BF16)


def placed(owner, live, half, slots):
    tokens = owner.shape[0]
    return pl.pallas_call(
        functools.partial(place_kernel, half),
        out_shape=[jax.ShapeDtypeStruct((slots // 2, tokens), BF16)] * 2,
    )(owner[None, :], owner[:, None], live[None, :])


def along_x(value):
    groups = [[SIDE * y + x for x in range(SIDE)] for y in range(SIDE)]
    return lax.all_to_all(value, "tp", 0, 0, tiled=True, axis_index_groups=groups)


def along_y(value):
    groups = [[SIDE * y + x for y in range(SIDE)] for x in range(SIDE)]
    return lax.all_to_all(value, "tp", 0, 0, tiled=True, axis_index_groups=groups)


def to_all(value):
    return jnp.broadcast_to(value, (SIDE,) + value.shape)


def side_by_side(left, right):
    groups = lax.axis_size("seq")
    both = jnp.concatenate([left, right], axis=0).astype(BF16).T
    return both.reshape(groups, both.shape[0] // groups, both.shape[1])


def exchange_rows(both):
    moved = lax.all_to_all(both, "seq", split_axis=0, concat_axis=0, tiled=True)
    return moved.reshape(-1, moved.shape[2])


def local(hidden, next_ids, live_mask, emb_table, gain_hidden, gain_embed, projection, target):
    width = hidden.shape[1]
    groups = lax.axis_size("seq")
    my_group = lax.axis_index("seq")
    place_tp = lax.axis_index("tp")
    my_y = place_tp // SIDE
    tokens = live_mask.shape[0]
    capacity = 2 * tokens // groups
    slots = groups * capacity
    row_count, local_width = emb_table.shape
    columns = projection.shape[1]
    quarter = width // SIDE

    hid_all = lax.all_gather(hidden, "tp", axis=0, tiled=True)

    def scale_row():
        hidden_f32 = hidden.astype(F32)
        own = lax.rsqrt(jnp.mean(hidden_f32 * hidden_f32, axis=-1) + 1e-06)
        rows_here = hidden.shape[0]
        lane = jnp.arange(tokens, dtype=I32)
        return jnp.where(lane // rows_here == place_tp, jnp.tile(own, tokens // rows_here), 0.0)

    proj_t = projection.T
    part = columns // CORES
    my_core = my_group % CORES

    def piece(y):
        return lax.dynamic_slice(proj_t, (my_core * part, width + y * quarter), (part, quarter))

    def fetch_half():
        fetched_half = jnp.zeros((SIDE, part, quarter), BF16)
        fetched_half = lax.dynamic_update_slice(fetched_half, piece(my_y)[None], (my_y, 0, 0))
        for step in range(1, SIDE):
            moved = lax.ppermute(
                piece((my_y + step) % SIDE),
                "tp",
                [(SIDE * y + x, SIDE * ((y + step) % SIDE) + x) for y in range(SIDE) for x in range(SIDE)],
            )
            fetched_half = lax.dynamic_update_slice(fetched_half, moved[None], ((my_y - step) % SIDE, 0, 0))
        fetched_half = fetched_half.reshape(SIDE * part, quarter)
        return fetched_half, lax.ppermute(fetched_half, "seq", [(k, k ^ 1) for k in range(groups)])

    first = my_core == 0

    def ordered(here, other):
        return jnp.where(first, here, other), jnp.where(first, other, here)

    ids_all = next_ids.reshape(groups, tokens)
    mine = ids_all // row_count == my_group
    token = jnp.arange(tokens, dtype=I32)
    upto = (token[:, None] <= token[None, :]).astype(BF16)
    rank_all = contract(mine.astype(BF16), upto, (1, 0)).astype(I32) - 1
    local_ids = ids_all - my_group * row_count
    half = capacity // 2
    row = jnp.arange(row_count, dtype=I32)

    def asked(first):
        ranks = first + jnp.arange(half, dtype=I32)
        hit = mine[:, None, :] & (rank_all[:, None, :] == ranks[None, :, None])
        return jnp.sum(jnp.where(hit, local_ids[:, None, :] + 1, 0), axis=2).reshape(slots // 2) - 1

    def picked(rows):
        return (row[:, None] == rows[None, :]).astype(BF16)

    rows_left, rows_right = asked(0), asked(half)
    table_t = emb_table.T

    ids_mine = lax.dynamic_index_in_dim(ids_all, my_group, 0, keepdims=False)
    owner = ids_mine // row_count
    wanted = side_by_side(contract(table_t, picked(rows_left), (1, 0)), contract(table_t, picked(rows_right), (1, 0)))

    def fetch():
        gain = lax.dynamic_slice_in_dim(gain_embed, place_tp * local_width, local_width)[:, None]
        return exchange_rows(wanted), *fetch_half(), gain, scale_row(), *placed(owner, live_mask, half, slots)

    def skip():
        return jax.tree.map(lambda leaf: jnp.zeros(leaf.shape, leaf.dtype), jax.eval_shape(fetch))

    fetched, weights_here, weights_other, gain, hidden_scale, place_left, place_right = lax.cond(my_group < groups, fetch, skip)

    emb = contract(fetched, place_left, (0, 0))[:local_width] + contract(fetched, place_right, (0, 0))[local_width:]
    squares = jnp.sum(emb * emb, axis=0, keepdims=True)
    shared = jnp.concatenate([squares, hidden_scale[None, :]], axis=0)
    message = jnp.concatenate([(emb * gain).astype(BF16), split_rows(shared)], axis=0)
    rows_of_devices = [[SIDE * y + x for x in range(SIDE)] for y in range(SIDE)]
    got = lax.all_gather(message, "tp", axis=0, tiled=False, axis_index_groups=rows_of_devices)
    shared = join_rows(got[:, local_width:], 2)
    features = got[:, :local_width].reshape(quarter, tokens)
    halves = ordered(contract(weights_here, features, (1, 0)), contract(weights_other, features, (1, 0)))
    halves = [half_rows.astype(BF16).reshape(SIDE, part, tokens) for half_rows in halves]
    got = along_y(jnp.concatenate([*halves, to_all(split_rows(shared))], axis=1))
    emb_raw = jnp.sum(got[:, :columns].astype(F32), axis=0)
    shared = join_rows(got[:, columns:], 2)
    scale = lax.rsqrt(shared[:1] / width + 1e-06)
    hidden_scale = shared[1:]

    hid_gained = (hid_all.astype(F32) * gain_hidden).astype(BF16)
    hid_raw = lax.optimization_barrier(contract(proj_t[:, :width], hid_gained, (1, 1)))
    combined = hid_raw * hidden_scale + emb_raw * scale
    projected = combined.astype(BF16)
    upstream = (combined - target.T.astype(F32)).astype(BF16)
    curve = jnp.sum(upstream.astype(F32) * emb_raw, axis=0, keepdims=True)
    got = along_y(to_all(jnp.concatenate([upstream, split_rows(curve)], axis=0)))
    curve = join_rows(got[:, columns:], 1)
    here, other = ordered(got[:, :part], got[:, part:columns])
    partial = contract(weights_here, here.reshape(SIDE * part, tokens), (0, 0))
    partial = partial + contract(weights_other, other.reshape(SIDE * part, tokens), (0, 0))
    partial = partial.astype(BF16).reshape(SIDE, local_width, tokens)
    got = along_x(jnp.concatenate([partial, to_all(split_rows(curve))], axis=1))
    feature_grad = jnp.sum(got[:, :local_width].astype(F32), axis=0)
    curvature = join_rows(got[:, local_width:], 1)

    emb_grad = scale * gain * feature_grad - scale * scale * scale * curvature / width * emb
    emb_grad = emb_grad.astype(BF16)
    returned = side_by_side(contract(emb_grad, place_left, (1, 1)), contract(emb_grad, place_right, (1, 1)))
    arrived = exchange_rows(returned)
    table_grad = (
        contract(arrived, picked(rows_left), (0, 1))[:local_width] + contract(arrived, picked(rows_right), (0, 1))[local_width:]
    ).astype(BF16)
    return (projected.T, table_grad.T)


def solution(mesh):
    return jax.shard_map(
        local,
        mesh=mesh,
        in_specs=(
            P(("seq", "tp"), None),
            P(),
            P("seq"),
            P("seq", "tp"),
            P(),
            P(),
            P(None, "tp"),
            P("seq", "tp"),
        ),
        out_specs=(P("seq", "tp"), P("seq", "tp")),
        check_vma=False,
    )
```
